256 devices in a mesh: seq: 32 (over y, x, core), head: 8 (over z).
Axes of the slice: x: 4, y: 4, z: 8, core: 2. Of those that a mesh axis runs over, the one named last changes fastest.
Arguments:
- queries: bfloat16 [32768, 32, 128], P('seq', 'head'), may hold values from -6 to 6
- key_vectors: bfloat16 [32768, 32, 128], P('seq', 'head'), may hold values from -6 to 6
- value_vectors: bfloat16 [32768, 32, 128], P('seq', 'head'), may hold values from -6 to 6
- out_grad: bfloat16 [32768, 32, 128], P(('seq', 'head')), may hold values from -6 to 6
Outputs:
- attended: bfloat16 [32768, 32, 128], P(('seq', 'head'))
- query_grad: bfloat16 [32768, 32, 128], P('seq', 'head')
- key_grad: bfloat16 [32768, 32, 128], P('seq', 'head')
- value_grad: bfloat16 [32768, 32, 128], P('seq', 'head')
The draws below stay inside these ranges and needn't reach their ends.
All inputs are finite; a program needn't handle non-finite values.
Results may differ from the reference program's by a relative error of at most 0.0058.
Values may be sent and summed in bfloat16 or wider, within the bound.
A program may use at most 128 MiB of HBM per device.

```python
import jax
import jax.numpy as jnp
from jax import lax

H = 32
HD = 128
TOK_DEV = 1024
TOKENS = 32768
N_SEQ = 32


def steps_of(rng, extent, pieces, least, largest):
    def one(dim, blocks):
        draws = jax.random.uniform(jax.random.fold_in(jax.random.fold_in(rng, 6), dim), (blocks,), jnp.float32, least / len(pieces), largest / len(pieces))
        return jnp.repeat(jnp.exp(draws), extent[dim] // blocks).reshape((-1,) + (1,) * (len(extent) - dim - 1))

    gain = one(*pieces[0])
    for cut in pieces[1:]:
        gain = gain * one(*cut)
    return gain


def scatter_about(key, extent, width, bound, shards=(), kind=jnp.bfloat16):
    factor_of = steps_of(key, extent, shards, -0.22, 0.18) if shards else 1.0
    values = jax.random.normal(key, extent, jnp.float32) * width * factor_of
    return jnp.minimum(jnp.maximum(values, -bound), bound).astype(kind)


def setup_inputs(seed: int = 0) -> dict:
    splits = jax.random.split(jax.random.key(seed), 5)
    queries = scatter_about(splits[0], (TOKENS, H, HD), 1.0, 6.0, ((0, 32), (1, 8)))
    key_vectors = scatter_about(splits[1], (TOKENS, H, HD), 1.0, 6.0, ((0, 32), (1, 8)))
    value_vectors = scatter_about(splits[2], (TOKENS, H, HD), 1.0, 6.0, ((0, 32), (1, 8)))
    out_grad = scatter_about(splits[3], (TOKENS, H, HD), 1.0, 6.0, ((0, 256),))
    return {"queries": queries, "key_vectors": key_vectors, "value_vectors": value_vectors, "out_grad": out_grad}


def bf_round(values):
    return lax.optimization_barrier(values.astype(jnp.bfloat16)).astype(jnp.float32)

def seg_scaling(seg_index):
    position = (seg_index * TOK_DEV + jnp.arange(TOK_DEV, dtype=jnp.int32)).astype(jnp.float32)
    return 1.0 / jnp.sqrt(HD * (position + 1.0))

def reference(queries, key_vectors, value_vectors, out_grad):
    shape_seg = (N_SEQ, TOK_DEV, H, HD)
    query_seg = queries.reshape(shape_seg)
    key_seg = key_vectors.reshape(shape_seg)
    value_seg = value_vectors.reshape(shape_seg)
    grad_seg = out_grad.reshape(shape_seg)
    seg_ids = jnp.arange(N_SEQ, dtype=jnp.int32)

    def states(items):
        query_part, key_part, value_part, grad_part, seg_index = items
        scaling = seg_scaling(seg_index)
        scaled_grad = (scaling[:, None, None] * grad_part.astype(jnp.float32)).astype(jnp.bfloat16)
        seg_state = jnp.einsum('shd,she->hde', key_part.astype(jnp.float32), value_part.astype(jnp.float32))
        grad_state = jnp.einsum('thd,the->hde', query_part.astype(jnp.float32), scaled_grad.astype(jnp.float32))
        return (seg_state, grad_state, scaled_grad)
    seg_state, grad_state, scaled_all = lax.map(states, (query_seg, key_seg, value_seg, grad_seg, seg_ids))
    zero_state = jnp.zeros((1, H, HD, HD), jnp.float32)
    prefix_all = jnp.concatenate([zero_state, jnp.cumsum(seg_state, axis=0)[:-1]], axis=0).astype(jnp.bfloat16)
    later_incl = jnp.flip(jnp.cumsum(jnp.flip(grad_state, 0), axis=0), 0)
    suffix_all = jnp.concatenate([later_incl[1:], zero_state], axis=0).astype(jnp.bfloat16)
    causal = (jnp.arange(TOK_DEV)[None, :] <= jnp.arange(TOK_DEV)[:, None])[None]

    def outputs(items):
        query_part, key_part, value_part, scaled_grad, prefix, suffix, seg_index = items
        scaling = seg_scaling(seg_index)
        query_f = query_part.astype(jnp.float32)
        key_f = key_part.astype(jnp.float32)
        value_f = value_part.astype(jnp.float32)
        grad_f = scaled_grad.astype(jnp.float32)
        prefix_f = prefix.astype(jnp.float32)
        suffix_f = suffix.astype(jnp.float32)
        within = bf_round(jnp.where(causal, jnp.einsum('thd,shd->hts', query_f, key_f), 0.0))
        grad_scores = bf_round(jnp.where(causal, jnp.einsum('thd,shd->hts', grad_f, value_f), 0.0))
        attended = scaling[:, None, None] * (jnp.einsum('thd,hde->the', query_f, prefix_f) + jnp.einsum('hts,shd->thd', within, value_f))
        query_grad = jnp.einsum('the,hde->thd', grad_f, prefix_f) + jnp.einsum('hts,shd->thd', grad_scores, key_f)
        key_grad = jnp.einsum('shj,hij->shi', value_f, suffix_f) + jnp.einsum('hts,thd->shd', grad_scores, query_f)
        value_grad = jnp.einsum('shi,hij->shj', key_f, suffix_f) + jnp.einsum('hts,the->she', within, grad_f)
        return (attended.astype(jnp.bfloat16), query_grad.astype(jnp.bfloat16), key_grad.astype(jnp.bfloat16), value_grad.astype(jnp.bfloat16))
    attended, query_grad, key_grad, value_grad = lax.map(outputs, (query_seg, key_seg, value_seg, scaled_all, prefix_all, suffix_all, seg_ids))
    full_shape = (N_SEQ * TOK_DEV, H, HD)
    return (attended.reshape(full_shape), query_grad.reshape(full_shape), key_grad.reshape(full_shape), value_grad.reshape(full_shape))
```

```python
import jax
import jax.numpy as jnp
from jax import lax
from jax.experimental import pallas as pl
from jax.experimental.pallas import tpu as pltpu
from jax.sharding import PartitionSpec as P

MESH = pl.DeviceIdType.MESH
BF = jnp.bfloat16
F32 = jnp.float32

NSEQ = 32
NHEAD = 8
TOK = 1024
HL = 4
D = 128
ROWS = TOK * HL
BLK = TOK // NHEAD
CH = 256
NCH = ROWS // CH
PIECE = HL * D // NSEQ
SEND_ORDER = (4, 3, 5, 2, 6, 1, 7)


def nn(a, b):
    return lax.dot_general(a, b, (((1,), (0,)), ((), ())), preferred_element_type=F32)


def nt(a, b):
    return lax.dot_general(a, b, (((1,), (1,)), ((), ())), preferred_element_type=F32)


def tn(a, b):
    return lax.dot_general(a, b, (((0,), (0,)), ((), ())), preferred_element_type=F32)


def kernel(
    q_hbm, k_hbm, v_hbm, g_hbm,
    att_hbm, qg_hbm, kg_hbm, vg_hbm,
    q_buf, k_buf, v_buf, g_land, gs_buf, att_buf,
    att_loc, kg_loc, vg_loc, qg_buf, kg_buf, vg_buf,
    k_run, g_run, p_chunk, within_t, scale_buf,
    head_mask, tri_mask, tri_mask_t,
    acc, state_buf, piece_in, piece_out, prefix_buf,
    gstate_buf, gpiece_in, gpiece_out, suffix_buf,
    load_sem, out_sem, z_send, z_recv, own_sem, scan_send, scan_recv,
):
    me = lax.axis_index("seq")
    z = lax.axis_index("head")

    loads = []
    for i, (src, dst) in enumerate(((k_hbm, k_buf), (v_hbm, v_buf), (q_hbm, q_buf))):
        copy = pltpu.make_async_copy(src, dst, load_sem.at[i])
        copy.start()
        loads.append(copy)

    barrier = pltpu.get_barrier_semaphore()
    for d in range(1, NHEAD):
        pl.semaphore_signal(
            barrier, inc=1, device_id={"head": lax.rem(z + d, NHEAD)}, device_id_type=MESH
        )

    def greet(d, carry):
        pl.semaphore_signal(
            barrier, inc=1, device_id={"seq": lax.rem(me + d, NSEQ)}, device_id_type=MESH
        )
        return carry

    lax.fori_loop(1, NSEQ, greet, 0)
    pl.semaphore_wait(barrier, NHEAD - 1 + NSEQ - 1)

    grad_in = []
    for d in SEND_ORDER:
        to = lax.rem(z + d, NHEAD)
        copy = pltpu.make_async_remote_copy(
            src_ref=g_hbm.at[:, to],
            dst_ref=g_land.at[pl.ds(z * BLK, BLK)],
            send_sem=z_send.at[d],
            recv_sem=z_recv.at[d],
            device_id={"head": to},
            device_id_type=MESH,
        )
        copy.start()
        grad_in.append(copy)
    own_grad = pltpu.make_async_copy(g_hbm.at[:, z], g_land.at[pl.ds(z * BLK, BLK)], own_sem.at[0])
    own_grad.start()

    row = lax.broadcasted_iota(jnp.int32, (CH, HL * D), 0)
    col = lax.broadcasted_iota(jnp.int32, (CH, HL * D), 1)
    head_mask[...] = ((row & 3) == (col >> 7)).astype(F32).astype(BF)
    row = lax.broadcasted_iota(jnp.int32, (CH, CH), 0)
    col = lax.broadcasted_iota(jnp.int32, (CH, CH), 1)
    same = (row & 3) == (col & 3)
    tri_mask[...] = (same & (col <= row)).astype(F32).astype(BF)
    tri_mask_t[...] = (same & (row <= col)).astype(F32).astype(BF)

    def rows(c):
        return pl.ds(pl.multiple_of(c * CH, CH), CH)

    def spread(x):
        return jnp.concatenate([x] * HL, axis=1) * head_mask[...]

    def wide(stacked):
        return jnp.concatenate([stacked[h * D : (h + 1) * D] for h in range(HL)], axis=1)

    def stack(w):
        return jnp.concatenate([w[:, h * D : (h + 1) * D] for h in range(HL)], axis=0)

    def each_chunk(body):
        lax.fori_loop(0, NCH, lambda c, carry: (body(c), carry)[1], 0)

    def scatter_pieces(src, dst, k):
        def one(d, carry):
            to = lax.rem(me + d, NSEQ)
            pltpu.make_async_remote_copy(
                src_ref=src.at[pl.ds(pl.multiple_of(to * PIECE, PIECE), PIECE)],
                dst_ref=dst.at[me],
                send_sem=scan_send.at[k],
                recv_sem=scan_recv.at[k],
                device_id={"seq": to},
                device_id_type=MESH,
            ).start()
            return carry

        lax.fori_loop(1, NSEQ, one, 0)
        dst[me] = src[pl.ds(pl.multiple_of(me * PIECE, PIECE), PIECE)]

    def return_pieces(src, dst, k):
        def one(d, carry):
            to = lax.rem(me + d, NSEQ)
            pltpu.make_async_remote_copy(
                src_ref=src.at[to],
                dst_ref=dst.at[pl.ds(pl.multiple_of(me * PIECE, PIECE), PIECE)],
                send_sem=scan_send.at[k],
                recv_sem=scan_recv.at[k],
                device_id={"seq": to},
                device_id_type=MESH,
            ).start()
            return carry

        lax.fori_loop(1, NSEQ, one, 0)
        dst[pl.ds(pl.multiple_of(me * PIECE, PIECE), PIECE)] = src[me]

    def wait_pieces(ref, sem):
        part = ref.at[pl.ds(0, NSEQ - 1)]
        pltpu.make_async_copy(part, part, sem).wait()

    def wait_rows(ref, sem):
        part = ref.at[pl.ds(0, (NSEQ - 1) * PIECE)]
        pltpu.make_async_copy(part, part, sem).wait()

    acc[...] = jnp.zeros_like(acc)
    loads[0].wait()
    loads[1].wait()

    def key_state(c):
        k_run[c] = acc[...]
        acc[...] += tn(k_buf[rows(c)], spread(v_buf[rows(c)]))

    each_chunk(key_state)
    state_buf[...] = stack(acc[...])
    scatter_pieces(state_buf, piece_in, 0)

    loads[2].wait()

    def local_attend(c):
        q, k = q_buf[rows(c)], k_buf[rows(c)]
        within = nt(q, k).astype(BF) * tri_mask[...]
        att_loc[rows(c)] = nn(within, v_buf[rows(c)])
        token = lax.broadcasted_iota(jnp.int32, (CH, D), 0) >> 2
        position = (me * TOK + c * (CH // HL) + token).astype(F32)
        scale_buf[rows(c)] = 1.0 / jnp.sqrt(D * (position + 1.0))

    each_chunk(local_attend)

    wait_pieces(piece_in, scan_recv.at[0])

    def scan_up(j, run):
        piece_out[j] = run.astype(BF)
        return run + piece_in[j]

    lax.fori_loop(0, NSEQ, scan_up, jnp.zeros((PIECE, D), F32))
    return_pieces(piece_out, prefix_buf, 1)

    def local_within_t(c):
        within_t[c] = nt(k_buf[rows(c)], q_buf[rows(c)]).astype(BF) * tri_mask_t[...]

    each_chunk(local_within_t)
    wait_rows(prefix_buf, scan_recv.at[1])

    att_rows = att_buf.reshape(ROWS, D)

    def attend(c):
        prefix = (prefix_buf[...].astype(F32) + stack(k_run[c])).astype(BF)
        p_chunk[c] = prefix
        total = att_loc[rows(c)] + nn(spread(q_buf[rows(c)]), prefix)
        att_rows[rows(c)] = (scale_buf[rows(c)] * total).astype(BF)

    each_chunk(attend)

    own_grad.wait()
    for copy in grad_in:
        copy.wait_recv()

    att_out = []
    for d in SEND_ORDER:
        to = lax.rem(z + d, NHEAD)
        copy = pltpu.make_async_remote_copy(
            src_ref=att_buf.at[pl.ds(to * BLK, BLK)],
            dst_ref=att_hbm.at[:, z],
            send_sem=z_send.at[NHEAD + d],
            recv_sem=z_recv.at[NHEAD + d],
            device_id={"head": to},
            device_id_type=MESH,
        )
        copy.start()
        att_out.append(copy)
    own_att = pltpu.make_async_copy(
        att_buf.at[pl.ds(z * BLK, BLK)], att_hbm.at[:, z], own_sem.at[1]
    )
    own_att.start()

    g_rows = g_land.reshape(ROWS, D)
    acc[...] = jnp.zeros_like(acc)

    def grad_state(i):
        c = NCH - 1 - i
        g = (scale_buf[rows(c)] * g_rows[rows(c)].astype(F32)).astype(BF)
        gs_buf[rows(c)] = g
        g_run[c] = acc[...]
        acc[...] += tn(q_buf[rows(c)], spread(g))

    each_chunk(grad_state)
    gstate_buf[...] = stack(acc[...])
    scatter_pieces(gstate_buf, gpiece_in, 2)

    def query_grad(c):
        g = gs_buf[rows(c)]
        scores = nt(g, v_buf[rows(c)]).astype(BF) * tri_mask[...]
        total = nt(spread(g), wide(p_chunk[c])) + nn(scores, k_buf[rows(c)])
        qg_buf[rows(c)] = total.astype(BF)

    each_chunk(query_grad)
    qg_out = pltpu.make_async_copy(qg_buf, qg_hbm, out_sem.at[0])
    qg_out.start()

    wait_pieces(gpiece_in, scan_recv.at[2])

    def scan_down(i, run):
        j = NSEQ - 1 - i
        gpiece_out[j] = run.astype(BF)
        return run + gpiece_in[j]

    lax.fori_loop(0, NSEQ, scan_down, jnp.zeros((PIECE, D), F32))
    return_pieces(gpiece_out, suffix_buf, 3)

    def local_key_value(c):
        g = gs_buf[rows(c)]
        scores_t = nt(v_buf[rows(c)], g).astype(BF) * tri_mask_t[...]
        kg_loc[rows(c)] = nn(scores_t, q_buf[rows(c)])
        vg_loc[rows(c)] = nn(within_t[c], g)

    each_chunk(local_key_value)
    wait_rows(suffix_buf, scan_recv.at[3])

    def key_value(c):
        suffix = (suffix_buf[...].astype(F32) + stack(g_run[c])).astype(BF)
        kg = kg_loc[rows(c)] + nt(spread(v_buf[rows(c)]), wide(suffix))
        kg_buf[rows(c)] = kg.astype(BF)
        vg = vg_loc[rows(c)] + nn(spread(k_buf[rows(c)]), suffix)
        vg_buf[rows(c)] = vg.astype(BF)

    each_chunk(key_value)
    kg_out = pltpu.make_async_copy(kg_buf, kg_hbm, out_sem.at[1])
    kg_out.start()
    vg_out = pltpu.make_async_copy(vg_buf, vg_hbm, out_sem.at[2])
    vg_out.start()

    wait_rows(state_buf, scan_send.at[0])
    wait_pieces(piece_out, scan_send.at[1])
    wait_rows(gstate_buf, scan_send.at[2])
    wait_pieces(gpiece_out, scan_send.at[3])
    for copy in grad_in:
        copy.wait_send()
    qg_out.wait()
    kg_out.wait()
    vg_out.wait()
    own_att.wait()
    for copy in att_out:
        copy.wait()


def per_device(queries, key_vectors, value_vectors, out_grad):
    flat = jax.ShapeDtypeStruct((ROWS, D), BF)
    hbm = pl.BlockSpec(memory_space=pltpu.HBM)
    vm = pltpu.VMEM
    dma = pltpu.SemaphoreType.DMA
    att, qg, kg, vg = pl.pallas_call(
        kernel,
        out_shape=(jax.ShapeDtypeStruct((BLK, NHEAD, HL, D), BF), flat, flat, flat),
        in_specs=[hbm] * 4,
        out_specs=[hbm] * 4,
        scratch_shapes=[
            vm((ROWS, D), BF), vm((ROWS, D), BF), vm((ROWS, D), BF),
            vm((TOK, HL, D), BF), vm((ROWS, D), BF), vm((TOK, HL, D), BF),
            vm((ROWS, D), F32), vm((ROWS, D), F32), vm((ROWS, D), F32),
            vm((ROWS, D), BF), vm((ROWS, D), BF), vm((ROWS, D), BF),
            vm((NCH, D, HL * D), F32), vm((NCH, D, HL * D), F32),
            vm((NCH, HL * D, D), BF), vm((NCH, CH, CH), BF), vm((ROWS, D), F32),
            vm((CH, HL * D), BF), vm((CH, CH), BF), vm((CH, CH), BF),
            vm((D, HL * D), F32),
            vm((HL * D, D), F32), vm((NSEQ, PIECE, D), F32), vm((NSEQ, PIECE, D), BF), vm((HL * D, D), BF),
            vm((HL * D, D), F32), vm((NSEQ, PIECE, D), F32), vm((NSEQ, PIECE, D), BF), vm((HL * D, D), BF),
            dma((3,)), dma((3,)), dma((2 * NHEAD,)), dma((2 * NHEAD,)), dma((2,)), dma((4,)), dma((4,)),
        ],
        compiler_params=pltpu.CompilerParams(
            collective_id=0, has_side_effects=True, vmem_limit_bytes=56 * 2**20
        ),
        cost_estimate=pl.CostEstimate(flops=16 * 10**9, bytes_accessed=8 * 2**20, transcendentals=0),
        name="attend",
    )(
        queries.reshape(ROWS, D),
        key_vectors.reshape(ROWS, D),
        value_vectors.reshape(ROWS, D),
        out_grad.reshape(BLK, NHEAD, HL, D),
    )
    shape = (TOK, HL, D)
    return (att.reshape(BLK, NHEAD * HL, D), qg.reshape(shape), kg.reshape(shape), vg.reshape(shape))


def solution(mesh):
    return jax.shard_map(
        per_device,
        mesh=mesh,
        in_specs=(
            P("seq", "head", None),
            P("seq", "head", None),
            P("seq", "head", None),
            P(("seq", "head"), None, None),
        ),
        out_specs=(
            P(("seq", "head"), None, None),
            P("seq", "head", None),
            P("seq", "head", None),
            P("seq", "head", None),
        ),
        check_vma=False,
    )
```

```python
import jax
import jax.numpy as jnp
from jax import lax
from jax.experimental import pallas as pl
from jax.experimental.pallas import tpu as pltpu
from jax.sharding import PartitionSpec as P

MESH = pl.DeviceIdType.MESH
BF = jnp.bfloat16
F32 = jnp.float32

NSEQ = 32
NHEAD = 8
TOK = 1024
HL = 4
D = 128
ROWS = TOK * HL
BLK = TOK // NHEAD
CH = 256
NCH = ROWS // CH
BLOCK = BLK * HL
PIECE = HL * D // NSEQ
SEND_ORDER = (4, 3, 5, 2, 6, 1, 7)


def nn(a, b):
    return lax.dot_general(a, b, (((1,), (0,)), ((), ())), preferred_element_type=F32)


def nt(a, b):
    return lax.dot_general(a, b, (((1,), (1,)), ((), ())), preferred_element_type=F32)


def tn(a, b):
    return lax.dot_general(a, b, (((0,), (0,)), ((), ())), preferred_element_type=F32)


def kernel(
    q_hbm, k_hbm, v_hbm, g_hbm,
    att_out_buf, qg_buf, kg_buf, vg_buf,
    q_buf, k_buf, v_buf, g_land, gs_buf, att_buf,
    att_loc, kg_loc, vg_loc,
    k_run, within_t, scale_buf,
    head_mask, tri_mask, tri_mask_t,
    acc, state_buf, piece_in, piece_out, prefix_buf,
    gstate_buf, gpiece_in, gpiece_out, suffix_buf,
    load_sem, z_send, z_recv, own_sem, scan_send, scan_recv,
):
    me = lax.axis_index("seq")
    z = lax.axis_index("head")

    loads = []
    for i, (src, dst) in enumerate(((k_hbm, k_buf), (v_hbm, v_buf), (q_hbm, q_buf))):
        copy = pltpu.make_async_copy(src, dst, load_sem.at[i])
        copy.start()
        loads.append(copy)

    barrier = pltpu.get_barrier_semaphore()
    for d in range(1, NHEAD):
        pl.semaphore_signal(
            barrier, inc=1, device_id={"head": lax.rem(z + d, NHEAD)}, device_id_type=MESH
        )

    def greet(d, carry):
        pl.semaphore_signal(
            barrier, inc=1, device_id={"seq": lax.rem(me + d, NSEQ)}, device_id_type=MESH
        )
        return carry

    lax.fori_loop(1, NSEQ, greet, 0)
    pl.semaphore_wait(barrier, NHEAD - 1 + NSEQ - 1)

    grad_in = []
    for d in SEND_ORDER:
        to = lax.rem(z + d, NHEAD)
        copy = pltpu.make_async_remote_copy(
            src_ref=g_hbm.at[:, to],
            dst_ref=g_land.at[pl.ds(z * BLK, BLK)],
            send_sem=z_send.at[d],
            recv_sem=z_recv.at[d],
            device_id={"head": to},
            device_id_type=MESH,
        )
        copy.start()
        grad_in.append(copy)
    own_grad = pltpu.make_async_copy(g_hbm.at[:, z], g_land.at[pl.ds(z * BLK, BLK)], own_sem.at[0])
    own_grad.start()

    row = lax.broadcasted_iota(jnp.int32, (CH, HL * D), 0)
    col = lax.broadcasted_iota(jnp.int32, (CH, HL * D), 1)
    for i in range(BLOCK // CH):
        head_mask[i * CH : (i + 1) * CH] = ((row & 3) == (col >> 7)).astype(F32).astype(BF)
    row = lax.broadcasted_iota(jnp.int32, (CH, CH), 0)
    col = lax.broadcasted_iota(jnp.int32, (CH, CH), 1)
    same = (row & 3) == (col & 3)
    tri_mask[...] = (same & (col <= row)).astype(F32).astype(BF)
    tri_mask_t[...] = (same & (row <= col)).astype(F32).astype(BF)

    def rows(c):
        return pl.ds(pl.multiple_of(c * CH, CH), CH)

    def spread(x):
        return jnp.concatenate([x] * HL, axis=1) * head_mask[: x.shape[0]]

    def wide(stacked):
        return jnp.concatenate([stacked[h * D : (h + 1) * D] for h in range(HL)], axis=1)

    def stack(w):
        return jnp.concatenate([w[:, h * D : (h + 1) * D] for h in range(HL)], axis=0)

    def each_chunk(body):
        lax.fori_loop(0, NCH, lambda c, carry: (body(c), carry)[1], 0, unroll=4)

    def scatter_pieces(src, dst, k):
        def one(d, carry):
            to = lax.rem(me + d, NSEQ)
            pltpu.make_async_remote_copy(
                src_ref=src.at[pl.ds(pl.multiple_of(to * PIECE, PIECE), PIECE)],
                dst_ref=dst.at[me],
                send_sem=scan_send.at[k],
                recv_sem=scan_recv.at[k],
                device_id={"seq": to},
                device_id_type=MESH,
            ).start()
            return carry

        lax.fori_loop(1, NSEQ, one, 0)
        dst[me] = src[pl.ds(pl.multiple_of(me * PIECE, PIECE), PIECE)]

    def return_pieces(src, dst, k):
        def one(d, carry):
            to = lax.rem(me + d, NSEQ)
            pltpu.make_async_remote_copy(
                src_ref=src.at[to],
                dst_ref=dst.at[pl.ds(pl.multiple_of(me * PIECE, PIECE), PIECE)],
                send_sem=scan_send.at[k],
                recv_sem=scan_recv.at[k],
                device_id={"seq": to},
                device_id_type=MESH,
            ).start()
            return carry

        lax.fori_loop(1, NSEQ, one, 0)
        dst[pl.ds(pl.multiple_of(me * PIECE, PIECE), PIECE)] = src[me]

    def wait_pieces(ref, sem):
        part = ref.at[pl.ds(0, NSEQ - 1)]
        pltpu.make_async_copy(part, part, sem).wait()

    def wait_rows(ref, sem):
        part = ref.at[pl.ds(0, (NSEQ - 1) * PIECE)]
        pltpu.make_async_copy(part, part, sem).wait()

    acc[...] = jnp.zeros_like(acc)
    loads[0].wait()
    loads[1].wait()

    def key_total(i, carry):
        part = pl.ds(pl.multiple_of(i * BLOCK, BLOCK), BLOCK)
        acc[...] += tn(k_buf[part], spread(v_buf[part]))
        return carry

    lax.fori_loop(0, ROWS // BLOCK, key_total, 0)
    state_buf[...] = stack(acc[...])
    scatter_pieces(state_buf, piece_in, 0)

    loads[2].wait()
    acc[...] = jnp.zeros_like(acc)

    def local_attend(c):
        q, k, v = q_buf[rows(c)], k_buf[rows(c)], v_buf[rows(c)]
        before = stack(acc[...])
        k_run[c] = before
        acc[...] += tn(k, spread(v))
        within = nt(q, k).astype(BF) * tri_mask[...]
        att_loc[rows(c)] = nn(within, v) + nn(spread(q), before.astype(BF))

    each_chunk(local_attend)

    wait_pieces(piece_in, scan_recv.at[0])

    def scan_up(j, run):
        piece_out[j] = run.astype(BF)
        return run + piece_in[j]

    lax.fori_loop(0, NSEQ, scan_up, jnp.zeros((PIECE, D), F32))
    return_pieces(piece_out, prefix_buf, 1)

    def local_within_t(c):
        within_t[c] = nt(k_buf[rows(c)], q_buf[rows(c)]).astype(BF) * tri_mask_t[...]
        token = lax.broadcasted_iota(jnp.int32, (CH, D), 0) >> 2
        position = (me * TOK + c * (CH // HL) + token).astype(F32)
        scale_buf[rows(c)] = 1.0 / jnp.sqrt(D * (position + 1.0))

    each_chunk(local_within_t)
    wait_rows(prefix_buf, scan_recv.at[1])

    att_rows = att_buf.reshape(ROWS, D)

    def attend(c):
        total = att_loc[rows(c)] + nn(spread(q_buf[rows(c)]), prefix_buf[...])
        att_rows[rows(c)] = (scale_buf[rows(c)] * total).astype(BF)

    each_chunk(attend)
    own_att = pltpu.make_async_copy(
        att_buf.at[pl.ds(z * BLK, BLK)], att_out_buf.at[:, z], own_sem.at[1]
    )
    own_att.start()

    g_rows = g_land.reshape(ROWS, D)
    acc[...] = jnp.zeros_like(acc)

    def grad_block(source):
        for half in range(BLOCK // CH):
            part = pl.ds(pl.multiple_of(source * BLOCK + half * CH, CH), CH)
            gs_buf[part] = (scale_buf[part] * g_rows[part].astype(F32)).astype(BF)
        part = pl.ds(pl.multiple_of(source * BLOCK, BLOCK), BLOCK)
        acc[...] += tn(q_buf[part], spread(gs_buf[part]))

    att_out = []

    def send_out(d):
        to = lax.rem(z + d, NHEAD)
        copy = pltpu.make_async_remote_copy(
            src_ref=att_buf.at[pl.ds(to * BLK, BLK)],
            dst_ref=att_out_buf.at[:, z],
            send_sem=z_send.at[NHEAD + d],
            recv_sem=z_recv.at[NHEAD + d],
            device_id={"head": to},
            device_id_type=MESH,
        )
        copy.start()
        att_out.append(copy)

    for d in SEND_ORDER[:2]:
        send_out(d)
    own_grad.wait()
    grad_block(z)
    for i, d in enumerate(SEND_ORDER):
        grad_in[i].wait_recv()
        for e in SEND_ORDER[i + 2 : i + 2 + 1]:
            send_out(e)
        grad_block(lax.rem(z + NHEAD - d, NHEAD))

    gstate_buf[...] = stack(acc[...])
    scatter_pieces(gstate_buf, gpiece_in, 2)

    def query_grad(c):
        g = gs_buf[rows(c)]
        prefix = (prefix_buf[...].astype(F32) + k_run[c]).astype(BF)
        scores = nt(g, v_buf[rows(c)]).astype(BF) * tri_mask[...]
        total = nt(spread(g), wide(prefix)) + nn(scores, k_buf[rows(c)])
        qg_buf[rows(c)] = total.astype(BF)

    each_chunk(query_grad)

    wait_pieces(gpiece_in, scan_recv.at[2])

    def scan_down(i, run):
        j = NSEQ - 1 - i
        gpiece_out[j] = run.astype(BF)
        return run + gpiece_in[j]

    lax.fori_loop(0, NSEQ, scan_down, jnp.zeros((PIECE, D), F32))
    return_pieces(gpiece_out, suffix_buf, 3)

    acc[...] = jnp.zeros_like(acc)

    def local_key_value(i):
        c = NCH - 1 - i
        g, q = gs_buf[rows(c)], q_buf[rows(c)]
        after = acc[...].astype(BF)
        acc[...] += tn(q, spread(g))
        scores_t = nt(v_buf[rows(c)], g).astype(BF) * tri_mask_t[...]
        kg_loc[rows(c)] = nn(scores_t, q) + nt(spread(v_buf[rows(c)]), after)
        vg_loc[rows(c)] = nn(within_t[c], g) + nn(spread(k_buf[rows(c)]), stack(after))

    each_chunk(local_key_value)
    wait_rows(suffix_buf, scan_recv.at[3])

    def key_value(c):
        suffix = suffix_buf[...]
        kg = kg_loc[rows(c)] + nt(spread(v_buf[rows(c)]), wide(suffix))
        kg_buf[rows(c)] = kg.astype(BF)
        vg = vg_loc[rows(c)] + nn(spread(k_buf[rows(c)]), suffix)
        vg_buf[rows(c)] = vg.astype(BF)

    each_chunk(key_value)

    wait_rows(state_buf, scan_send.at[0])
    wait_pieces(piece_out, scan_send.at[1])
    wait_rows(gstate_buf, scan_send.at[2])
    wait_pieces(gpiece_out, scan_send.at[3])
    for copy in grad_in:
        copy.wait_send()
    own_att.wait()
    for copy in att_out:
        copy.wait()


def store_kernel(*refs):
    sources, targets, sem = refs[:4], refs[4:8], refs[8]
    copies = [pltpu.make_async_copy(sources[i], targets[i], sem.at[i]) for i in range(4)]
    for copy in copies:
        copy.start()
    for copy in copies:
        copy.wait()


def per_device(queries, key_vectors, value_vectors, out_grad):
    hbm = pl.BlockSpec(memory_space=pltpu.HBM)
    vm = pltpu.VMEM
    in_vmem = pl.BlockSpec(memory_space=vm)
    dma = pltpu.SemaphoreType.DMA
    held = pl.pallas_call(
        kernel,
        out_shape=(vm((BLK, NHEAD, HL, D), BF), vm((ROWS, D), BF), vm((ROWS, D), BF), vm((ROWS, D), BF)),
        in_specs=[hbm] * 4,
        out_specs=[in_vmem] * 4,
        scratch_shapes=[
            vm((ROWS, D), BF), vm((ROWS, D), BF), vm((ROWS, D), BF),
            vm((TOK, HL, D), BF), vm((ROWS, D), BF), vm((TOK, HL, D), BF),
            vm((ROWS, D), F32), vm((ROWS, D), F32), vm((ROWS, D), F32),
            vm((NCH, HL * D, D), F32), vm((NCH, CH, CH), BF), vm((ROWS, D), F32),
            vm((BLOCK, HL * D), BF), vm((CH, CH), BF), vm((CH, CH), BF),
            vm((D, HL * D), F32),
            vm((HL * D, D), F32), vm((NSEQ, PIECE, D), F32), vm((NSEQ, PIECE, D), BF), vm((HL * D, D), BF),
            vm((HL * D, D), F32), vm((NSEQ, PIECE, D), F32), vm((NSEQ, PIECE, D), BF), vm((HL * D, D), BF),
            dma((3,)), dma((2 * NHEAD,)), dma((2 * NHEAD,)), dma((2,)), dma((4,)), dma((4,)),
        ],
        compiler_params=pltpu.CompilerParams(
            collective_id=0, has_side_effects=True, vmem_limit_bytes=56 * 2**20
        ),
        cost_estimate=pl.CostEstimate(flops=16 * 10**9, bytes_accessed=8 * 2**20, transcendentals=0),
        name="attend",
    )(
        queries.reshape(ROWS, D),
        key_vectors.reshape(ROWS, D),
        value_vectors.reshape(ROWS, D),
        out_grad.reshape(BLK, NHEAD, HL, D),
    )
    att, qg, kg, vg = pl.pallas_call(
        store_kernel,
        out_shape=[jax.ShapeDtypeStruct(x.shape, x.dtype) for x in held],
        in_specs=[pl.BlockSpec(memory_space=pl.ANY)] * 4,
        out_specs=[hbm] * 4,
        scratch_shapes=[dma((4,))],
        compiler_params=pltpu.CompilerParams(vmem_limit_bytes=2**20),
        name="store",
    )(*held)
    shape = (TOK, HL, D)
    return (att.reshape(BLK, NHEAD * HL, D), qg.reshape(shape), kg.reshape(shape), vg.reshape(shape))


def solution(mesh):
    return jax.shard_map(
        per_device,
        mesh=mesh,
        in_specs=(
            P("seq", "head", None),
            P("seq", "head", None),
            P("seq", "head", None),
            P(("seq", "head"), None, None),
        ),
        out_specs=(
            P(("seq", "head"), None, None),
            P("seq", "head", None),
            P("seq", "head", None),
            P("seq", "head", None),
        ),
        check_vma=False,
    )
```

```python
import jax
import jax.numpy as jnp
from jax import lax
from jax.experimental import pallas as pl
from jax.experimental.pallas import tpu as pltpu
from jax.sharding import PartitionSpec as P

MESH = pl.DeviceIdType.MESH
BF = jnp.bfloat16
F32 = jnp.float32

NSEQ = 32
NHEAD = 8
TOK = 1024
HL = 4
D = 128
ROWS = TOK * HL
BLK = TOK // NHEAD
CH = 256
NCH = ROWS // CH
BLOCK = BLK * HL
PIECE = HL * D // NSEQ
GATE = 3
SEND_ORDER = (4, 3, 5, 2, 6, 1, 7)


def nn(a, b):
    return lax.dot_general(a, b, (((1,), (0,)), ((), ())), preferred_element_type=F32)


def nt(a, b):
    return lax.dot_general(a, b, (((1,), (1,)), ((), ())), preferred_element_type=F32)


def tn(a, b):
    return lax.dot_general(a, b, (((0,), (0,)), ((), ())), preferred_element_type=F32)


def kernel(
    q_hbm, k_hbm, v_hbm, g_hbm,
    att_out_buf, qg_buf, kg_buf, vg_buf,
    q_buf, k_buf, v_buf, g_land, gs_buf, att_buf,
    att_loc, kg_loc, vg_loc,
    k_run, within_t, scale_buf,
    head_mask, tri_mask, tri_mask_t,
    acc, state_buf, piece_in, piece_out, prefix_buf,
    gstate_buf, gpiece_in, gpiece_out, suffix_buf,
    load_sem, z_send, z_recv, own_sem, scan_send, scan_recv, column_in, all_in,
):
    me = lax.axis_index("seq")
    z = lax.axis_index("head")

    loads = []
    for i, (src, dst) in enumerate(((k_hbm, k_buf), (v_hbm, v_buf), (q_hbm, q_buf))):
        copy = pltpu.make_async_copy(src, dst, load_sem.at[i])
        copy.start()
        loads.append(copy)

    barrier = pltpu.get_barrier_semaphore()
    for d in range(1, NHEAD):
        to = lax.rem(z + d, NHEAD)

        @pl.when(to != GATE)
        def _():
            pl.semaphore_signal(barrier, inc=1, device_id={"head": to}, device_id_type=MESH)

    @pl.when(z != GATE)
    def _():
        pl.semaphore_wait(barrier, NHEAD - 1)

    @pl.when(z == GATE + 1)
    def _():
        pl.semaphore_signal(column_in, inc=1, device_id={"head": GATE}, device_id_type=MESH)

    @pl.when(z == GATE)
    def _():
        pl.semaphore_wait(column_in, 1)

    grad_in = []
    for d in SEND_ORDER:
        to = lax.rem(z + d, NHEAD)
        copy = pltpu.make_async_remote_copy(
            src_ref=g_hbm.at[:, to],
            dst_ref=g_land.at[pl.ds(z * BLK, BLK)],
            send_sem=z_send.at[d],
            recv_sem=z_recv.at[d],
            device_id={"head": to},
            device_id_type=MESH,
        )
        copy.start()
        grad_in.append(copy)
    own_grad = pltpu.make_async_copy(g_hbm.at[:, z], g_land.at[pl.ds(z * BLK, BLK)], own_sem.at[0])
    own_grad.start()

    @pl.when(z == GATE)
    def _():
        def greet(d, carry):
            pl.semaphore_signal(
                barrier, inc=1, device_id={"seq": lax.rem(me + d, NSEQ)}, device_id_type=MESH
            )
            return carry

        lax.fori_loop(1, NSEQ, greet, 0)

    row = lax.broadcasted_iota(jnp.int32, (CH, HL * D), 0)
    col = lax.broadcasted_iota(jnp.int32, (CH, HL * D), 1)
    for i in range(BLOCK // CH):
        head_mask[i * CH : (i + 1) * CH] = ((row & 3) == (col >> 7)).astype(F32).astype(BF)
    row = lax.broadcasted_iota(jnp.int32, (CH, CH), 0)
    col = lax.broadcasted_iota(jnp.int32, (CH, CH), 1)
    same = (row & 3) == (col & 3)
    tri_mask[...] = (same & (col <= row)).astype(F32).astype(BF)
    tri_mask_t[...] = (same & (row <= col)).astype(F32).astype(BF)

    def rows(c):
        return pl.ds(pl.multiple_of(c * CH, CH), CH)

    def spread(x):
        return jnp.concatenate([x] * HL, axis=1) * head_mask[: x.shape[0]]

    def wide(stacked):
        return jnp.concatenate([stacked[h * D : (h + 1) * D] for h in range(HL)], axis=1)

    def stack(w):
        return jnp.concatenate([w[:, h * D : (h + 1) * D] for h in range(HL)], axis=0)

    def each_chunk(body, unroll=4):
        lax.fori_loop(0, NCH, lambda c, carry: (body(c), carry)[1], 0, unroll=unroll)

    def scatter_pieces(src, dst, k):
        def one(d, carry):
            to = lax.rem(me + d, NSEQ)
            pltpu.make_async_remote_copy(
                src_ref=src.at[pl.ds(pl.multiple_of(to * PIECE, PIECE), PIECE)],
                dst_ref=dst.at[me],
                send_sem=scan_send.at[k],
                recv_sem=scan_recv.at[k],
                device_id={"seq": to},
                device_id_type=MESH,
            ).start()
            return carry

        lax.fori_loop(1, NSEQ, one, 0)
        dst[me] = src[pl.ds(pl.multiple_of(me * PIECE, PIECE), PIECE)]

    def return_pieces(src, dst, k):
        def one(d, carry):
            to = lax.rem(me + d, NSEQ)
            pltpu.make_async_remote_copy(
                src_ref=src.at[to],
                dst_ref=dst.at[pl.ds(pl.multiple_of(me * PIECE, PIECE), PIECE)],
                send_sem=scan_send.at[k],
                recv_sem=scan_recv.at[k],
                device_id={"seq": to},
                device_id_type=MESH,
            ).start()
            return carry

        lax.fori_loop(1, NSEQ, one, 0)
        dst[pl.ds(pl.multiple_of(me * PIECE, PIECE), PIECE)] = src[me]

    def wait_pieces(ref, sem):
        part = ref.at[pl.ds(0, NSEQ - 1)]
        pltpu.make_async_copy(part, part, sem).wait()

    def wait_rows(ref, sem):
        part = ref.at[pl.ds(0, (NSEQ - 1) * PIECE)]
        pltpu.make_async_copy(part, part, sem).wait()

    acc[...] = jnp.zeros_like(acc)
    loads[0].wait()
    loads[1].wait()

    def key_total(i, carry):
        part = pl.ds(pl.multiple_of(i * BLOCK, BLOCK), BLOCK)
        acc[...] += tn(k_buf[part], spread(v_buf[part]))
        return carry

    lax.fori_loop(0, ROWS // BLOCK, key_total, 0)
    state_buf[...] = stack(acc[...])

    @pl.when(z == GATE)
    def _():
        pl.semaphore_wait(barrier, NSEQ - 1)
        for d in range(1, NHEAD):
            pl.semaphore_signal(
                all_in, inc=1, device_id={"head": lax.rem(z + d, NHEAD)}, device_id_type=MESH
            )

    @pl.when(z != GATE)
    def _():
        pl.semaphore_wait(all_in, 1)

    scatter_pieces(state_buf, piece_in, 0)

    loads[2].wait()
    acc[...] = jnp.zeros_like(acc)

    def local_attend(c):
        q, k, v = q_buf[rows(c)], k_buf[rows(c)], v_buf[rows(c)]
        before = stack(acc[...])
        k_run[c] = before
        acc[...] += tn(k, spread(v))
        within = nt(q, k).astype(BF) * tri_mask[...]
        att_loc[rows(c)] = nn(within, v) + nn(spread(q), before.astype(BF))

    each_chunk(local_attend)

    wait_pieces(piece_in, scan_recv.at[0])

    def scan_up(j, run):
        piece_out[j] = run.astype(BF)
        return run + piece_in[j]

    lax.fori_loop(0, NSEQ, scan_up, jnp.zeros((PIECE, D), F32))
    return_pieces(piece_out, prefix_buf, 1)

    def local_within_t(c):
        within_t[c] = nt(k_buf[rows(c)], q_buf[rows(c)]).astype(BF) * tri_mask_t[...]
        token = lax.broadcasted_iota(jnp.int32, (CH, D), 0) >> 2
        position = (me * TOK + c * (CH // HL) + token).astype(F32)
        scale_buf[rows(c)] = 1.0 / jnp.sqrt(D * (position + 1.0))

    each_chunk(local_within_t)
    wait_rows(prefix_buf, scan_recv.at[1])

    att_rows = att_buf.reshape(ROWS, D)

    def attend(c):
        total = att_loc[rows(c)] + nn(spread(q_buf[rows(c)]), prefix_buf[...])
        att_rows[rows(c)] = (scale_buf[rows(c)] * total).astype(BF)

    each_chunk(attend)
    own_att = pltpu.make_async_copy(
        att_buf.at[pl.ds(z * BLK, BLK)], att_out_buf.at[:, z], own_sem.at[1]
    )
    own_att.start()

    g_rows = g_land.reshape(ROWS, D)
    acc[...] = jnp.zeros_like(acc)

    def grad_block(source):
        for half in range(BLOCK // CH):
            part = pl.ds(pl.multiple_of(source * BLOCK + half * CH, CH), CH)
            gs_buf[part] = (scale_buf[part] * g_rows[part].astype(F32)).astype(BF)
        part = pl.ds(pl.multiple_of(source * BLOCK, BLOCK), BLOCK)
        acc[...] += tn(q_buf[part], spread(gs_buf[part]))

    att_out = []

    def send_out(d):
        to = lax.rem(z + d, NHEAD)
        copy = pltpu.make_async_remote_copy(
            src_ref=att_buf.at[pl.ds(to * BLK, BLK)],
            dst_ref=att_out_buf.at[:, z],
            send_sem=z_send.at[NHEAD + d],
            recv_sem=z_recv.at[NHEAD + d],
            device_id={"head": to},
            device_id_type=MESH,
        )
        copy.start()
        att_out.append(copy)

    for d in SEND_ORDER[:2]:
        send_out(d)
    own_grad.wait()
    grad_block(z)
    for i, d in enumerate(SEND_ORDER):
        grad_in[i].wait_recv()
        for e in SEND_ORDER[i + 2 : i + 2 + 1]:
            send_out(e)
        grad_block(lax.rem(z + NHEAD - d, NHEAD))

    gstate_buf[...] = stack(acc[...])
    scatter_pieces(gstate_buf, gpiece_in, 2)

    def query_grad(c):
        g = gs_buf[rows(c)]
        prefix = (prefix_buf[...].astype(F32) + k_run[c]).astype(BF)
        scores = nt(g, v_buf[rows(c)]).astype(BF) * tri_mask[...]
        total = nt(spread(g), wide(prefix)) + nn(scores, k_buf[rows(c)])
        qg_buf[rows(c)] = total.astype(BF)

    each_chunk(query_grad, 8)

    wait_pieces(gpiece_in, scan_recv.at[2])

    def scan_down(i, run):
        j = NSEQ - 1 - i
        gpiece_out[j] = run.astype(BF)
        return run + gpiece_in[j]

    lax.fori_loop(0, NSEQ, scan_down, jnp.zeros((PIECE, D), F32))
    return_pieces(gpiece_out, suffix_buf, 3)

    acc[...] = jnp.zeros_like(acc)

    def local_key_value(i):
        c = NCH - 1 - i
        g, q = gs_buf[rows(c)], q_buf[rows(c)]
        after = acc[...].astype(BF)
        acc[...] += tn(q, spread(g))
        scores_t = nt(v_buf[rows(c)], g).astype(BF) * tri_mask_t[...]
        kg_loc[rows(c)] = nn(scores_t, q) + nt(spread(v_buf[rows(c)]), after)
        vg_loc[rows(c)] = nn(within_t[c], g) + nn(spread(k_buf[rows(c)]), stack(after))

    each_chunk(local_key_value, 8)
    wait_rows(suffix_buf, scan_recv.at[3])

    def key_value(c):
        suffix = suffix_buf[...]
        kg = kg_loc[rows(c)] + nt(spread(v_buf[rows(c)]), wide(suffix))
        kg_buf[rows(c)] = kg.astype(BF)
        vg = vg_loc[rows(c)] + nn(spread(k_buf[rows(c)]), suffix)
        vg_buf[rows(c)] = vg.astype(BF)

    each_chunk(key_value, 8)

    wait_rows(state_buf, scan_send.at[0])
    wait_pieces(piece_out, scan_send.at[1])
    wait_rows(gstate_buf, scan_send.at[2])
    wait_pieces(gpiece_out, scan_send.at[3])
    for copy in grad_in:
        copy.wait_send()
    own_att.wait()
    for copy in att_out:
        copy.wait()


def store_kernel(*refs):
    sources, targets, sem = refs[:4], refs[4:8], refs[8]
    copies = [pltpu.make_async_copy(sources[i], targets[i], sem.at[i]) for i in range(4)]
    for copy in copies:
        copy.start()
    for copy in copies:
        copy.wait()


def per_device(queries, key_vectors, value_vectors, out_grad):
    hbm = pl.BlockSpec(memory_space=pltpu.HBM)
    vm = pltpu.VMEM
    in_vmem = pl.BlockSpec(memory_space=vm)
    dma = pltpu.SemaphoreType.DMA
    held = pl.pallas_call(
        kernel,
        out_shape=(vm((BLK, NHEAD, HL, D), BF), vm((ROWS, D), BF), vm((ROWS, D), BF), vm((ROWS, D), BF)),
        in_specs=[hbm] * 4,
        out_specs=[in_vmem] * 4,
        scratch_shapes=[
            vm((ROWS, D), BF), vm((ROWS, D), BF), vm((ROWS, D), BF),
            vm((TOK, HL, D), BF), vm((ROWS, D), BF), vm((TOK, HL, D), BF),
            vm((ROWS, D), F32), vm((ROWS, D), F32), vm((ROWS, D), F32),
            vm((NCH, HL * D, D), F32), vm((NCH, CH, CH), BF), vm((ROWS, D), F32),
            vm((BLOCK, HL * D), BF), vm((CH, CH), BF), vm((CH, CH), BF),
            vm((D, HL * D), F32),
            vm((HL * D, D), F32), vm((NSEQ, PIECE, D), F32), vm((NSEQ, PIECE, D), BF), vm((HL * D, D), BF),
            vm((HL * D, D), F32), vm((NSEQ, PIECE, D), F32), vm((NSEQ, PIECE, D), BF), vm((HL * D, D), BF),
            dma((3,)), dma((2 * NHEAD,)), dma((2 * NHEAD,)), dma((2,)), dma((4,)), dma((4,)),
            pltpu.SemaphoreType.REGULAR, pltpu.SemaphoreType.REGULAR,
        ],
        compiler_params=pltpu.CompilerParams(
            collective_id=0, has_side_effects=True, vmem_limit_bytes=56 * 2**20
        ),
        cost_estimate=pl.CostEstimate(flops=16 * 10**9, bytes_accessed=8 * 2**20, transcendentals=0),
        name="attend",
    )(
        queries.reshape(ROWS, D),
        key_vectors.reshape(ROWS, D),
        value_vectors.reshape(ROWS, D),
        out_grad.reshape(BLK, NHEAD, HL, D),
    )
    att, qg, kg, vg = pl.pallas_call(
        store_kernel,
        out_shape=[jax.ShapeDtypeStruct(x.shape, x.dtype) for x in held],
        in_specs=[pl.BlockSpec(memory_space=pl.ANY)] * 4,
        out_specs=[hbm] * 4,
        scratch_shapes=[dma((4,))],
        compiler_params=pltpu.CompilerParams(vmem_limit_bytes=2**20),
        name="store",
    )(*held)
    shape = (TOK, HL, D)
    return (att.reshape(BLK, NHEAD * HL, D), qg.reshape(shape), kg.reshape(shape), vg.reshape(shape))


def solution(mesh):
    return jax.shard_map(
        per_device,
        mesh=mesh,
        in_specs=(
            P("seq", "head", None),
            P("seq", "head", None),
            P("seq", "head", None),
            P(("seq", "head"), None, None),
        ),
        out_specs=(
            P(("seq", "head"), None, None),
            P("seq", "head", None),
            P("seq", "head", None),
            P("seq", "head", None),
        ),
        check_vma=False,
    )
```

```python
import jax
import jax.numpy as jnp
from jax import lax
from jax.experimental import pallas as pl
from jax.experimental.pallas import tpu as pltpu
from jax.sharding import PartitionSpec as P

MESH = pl.DeviceIdType.MESH
BF = jnp.bfloat16
F32 = jnp.float32

NSEQ = 32
NHEAD = 8
TOK = 1024
HL = 4
D = 128
ROWS = TOK * HL
BLK = TOK // NHEAD
CH = 256
NCH = ROWS // CH
BLOCK = BLK * HL
PIECE = HL * D // NSEQ
GATE = 3
HOLD = 4
SEND_ORDER = (4, 3, 5, 2, 6, 1, 7)


def nn(a, b):
    return lax.dot_general(a, b, (((1,), (0,)), ((), ())), preferred_element_type=F32)


def nt(a, b):
    return lax.dot_general(a, b, (((1,), (1,)), ((), ())), preferred_element_type=F32)


def tn(a, b):
    return lax.dot_general(a, b, (((0,), (0,)), ((), ())), preferred_element_type=F32)


def kernel(
    q_hbm, k_hbm, v_hbm, g_hbm,
    att_out_buf, qg_buf, kg_buf, vg_buf,
    q_buf, k_buf, v_buf, g_land, gs_buf, att_buf,
    att_loc, kg_loc, vg_loc,
    k_run, within_t, scale_buf,
    head_mask, tri_mask, tri_mask_t,
    acc, state_buf, piece_in, piece_out, prefix_buf,
    gstate_buf, gpiece_in, gpiece_out, suffix_buf,
    load_sem, z_send, z_recv, own_sem, scan_send, scan_recv, column_in, all_in,
):
    me = lax.axis_index("seq")
    z = lax.axis_index("head")

    loads = []
    for i, (src, dst) in enumerate(((k_hbm, k_buf), (v_hbm, v_buf), (q_hbm, q_buf))):
        copy = pltpu.make_async_copy(src, dst, load_sem.at[i])
        copy.start()
        loads.append(copy)

    barrier = pltpu.get_barrier_semaphore()
    for d in range(1, NHEAD):
        to = lax.rem(z + d, NHEAD)

        @pl.when(to != GATE)
        def _():
            pl.semaphore_signal(barrier, inc=1, device_id={"head": to}, device_id_type=MESH)

    @pl.when(z != GATE)
    def _():
        pl.semaphore_wait(barrier, NHEAD - 1)

    @pl.when(z == GATE + 1)
    def _():
        pl.semaphore_signal(column_in, inc=1, device_id={"head": GATE}, device_id_type=MESH)

    @pl.when(z == GATE)
    def _():
        pl.semaphore_wait(column_in, 1)

    grad_in = []
    for d in SEND_ORDER:
        to = lax.rem(z + d, NHEAD)
        copy = pltpu.make_async_remote_copy(
            src_ref=g_hbm.at[:, to],
            dst_ref=g_land.at[pl.ds(z * BLK, BLK)],
            send_sem=z_send.at[d],
            recv_sem=z_recv.at[d],
            device_id={"head": to},
            device_id_type=MESH,
        )
        copy.start()
        grad_in.append(copy)
    own_grad = pltpu.make_async_copy(g_hbm.at[:, z], g_land.at[pl.ds(z * BLK, BLK)], own_sem.at[0])
    own_grad.start()

    @pl.when(z == GATE)
    def _():
        def greet(d, carry):
            pl.semaphore_signal(
                barrier, inc=1, device_id={"seq": lax.rem(me + d, NSEQ)}, device_id_type=MESH
            )
            return carry

        lax.fori_loop(1, NSEQ, greet, 0)

    row = lax.broadcasted_iota(jnp.int32, (CH, HL * D), 0)
    col = lax.broadcasted_iota(jnp.int32, (CH, HL * D), 1)
    for i in range(BLOCK // CH):
        head_mask[i * CH : (i + 1) * CH] = ((row & 3) == (col >> 7)).astype(F32).astype(BF)
    row = lax.broadcasted_iota(jnp.int32, (CH, CH), 0)
    col = lax.broadcasted_iota(jnp.int32, (CH, CH), 1)
    same = (row & 3) == (col & 3)
    tri_mask[...] = (same & (col <= row)).astype(F32).astype(BF)
    tri_mask_t[...] = (same & (row <= col)).astype(F32).astype(BF)

    def rows(c):
        return pl.ds(pl.multiple_of(c * CH, CH), CH)

    def spread(x):
        return jnp.concatenate([x] * HL, axis=1) * head_mask[: x.shape[0]]

    def wide(stacked):
        return jnp.concatenate([stacked[h * D : (h + 1) * D] for h in range(HL)], axis=1)

    def stack(w):
        return jnp.concatenate([w[:, h * D : (h + 1) * D] for h in range(HL)], axis=0)

    def each_chunk(body, unroll=4):
        lax.fori_loop(0, NCH, lambda c, carry: (body(c), carry)[1], 0, unroll=unroll)

    def scatter_pieces(src, dst, k):
        def one(d, carry):
            to = lax.rem(me + d, NSEQ)
            pltpu.make_async_remote_copy(
                src_ref=src.at[pl.ds(pl.multiple_of(to * PIECE, PIECE), PIECE)],
                dst_ref=dst.at[me],
                send_sem=scan_send.at[k],
                recv_sem=scan_recv.at[k],
                device_id={"seq": to},
                device_id_type=MESH,
            ).start()
            return carry

        lax.fori_loop(1, NSEQ, one, 0)
        dst[me] = src[pl.ds(pl.multiple_of(me * PIECE, PIECE), PIECE)]

    def return_pieces(src, dst, k):
        def one(d, carry):
            to = lax.rem(me + d, NSEQ)
            pltpu.make_async_remote_copy(
                src_ref=src.at[to],
                dst_ref=dst.at[pl.ds(pl.multiple_of(me * PIECE, PIECE), PIECE)],
                send_sem=scan_send.at[k],
                recv_sem=scan_recv.at[k],
                device_id={"seq": to},
                device_id_type=MESH,
            ).start()
            return carry

        lax.fori_loop(1, NSEQ, one, 0)
        dst[pl.ds(pl.multiple_of(me * PIECE, PIECE), PIECE)] = src[me]

    def wait_pieces(ref, sem):
        part = ref.at[pl.ds(0, NSEQ - 1)]
        pltpu.make_async_copy(part, part, sem).wait()

    def wait_rows(ref, sem):
        part = ref.at[pl.ds(0, (NSEQ - 1) * PIECE)]
        pltpu.make_async_copy(part, part, sem).wait()

    acc[...] = jnp.zeros_like(acc)
    loads[0].wait()
    loads[1].wait()

    def key_total(i, carry):
        part = pl.ds(pl.multiple_of(i * BLOCK, BLOCK), BLOCK)
        acc[...] += tn(k_buf[part], spread(v_buf[part]))
        return carry

    lax.fori_loop(0, ROWS // BLOCK, key_total, 0)
    state_buf[...] = stack(acc[...])

    @pl.when(z == GATE)
    def _():
        pl.semaphore_wait(barrier, NSEQ - 1)
        for d in range(1, NHEAD):
            pl.semaphore_signal(
                all_in, inc=1, device_id={"head": lax.rem(z + d, NHEAD)}, device_id_type=MESH
            )

    @pl.when(z != GATE)
    def _():
        pl.semaphore_wait(all_in, 1)

    scatter_pieces(state_buf, piece_in, 0)

    loads[2].wait()
    acc[...] = jnp.zeros_like(acc)

    def local_attend(c):
        q, k, v = q_buf[rows(c)], k_buf[rows(c)], v_buf[rows(c)]
        before = stack(acc[...])
        k_run[c] = before
        acc[...] += tn(k, spread(v))
        within = nt(q, k).astype(BF) * tri_mask[...]
        att_loc[rows(c)] = nn(within, v) + nn(spread(q), before.astype(BF))

    each_chunk(local_attend)

    wait_pieces(piece_in, scan_recv.at[0])

    def scan_up(j, run):
        piece_out[j] = run.astype(BF)
        return run + piece_in[j]

    lax.fori_loop(0, NSEQ, scan_up, jnp.zeros((PIECE, D), F32))
    return_pieces(piece_out, prefix_buf, 1)

    def local_within_t(c):
        within_t[c] = nt(k_buf[rows(c)], q_buf[rows(c)]).astype(BF) * tri_mask_t[...]
        token = lax.broadcasted_iota(jnp.int32, (CH, D), 0) >> 2
        position = (me * TOK + c * (CH // HL) + token).astype(F32)
        scale_buf[rows(c)] = 1.0 / jnp.sqrt(D * (position + 1.0))

    each_chunk(local_within_t)
    wait_rows(prefix_buf, scan_recv.at[1])

    att_rows = att_buf.reshape(ROWS, D)

    def attend(c):
        total = att_loc[rows(c)] + nn(spread(q_buf[rows(c)]), prefix_buf[...])
        att_rows[rows(c)] = (scale_buf[rows(c)] * total).astype(BF)

    each_chunk(attend)
    own_att = pltpu.make_async_copy(
        att_buf.at[pl.ds(z * BLK, BLK)], att_out_buf.at[:, z], own_sem.at[1]
    )
    own_att.start()

    g_rows = g_land.reshape(ROWS, D)
    acc[...] = jnp.zeros_like(acc)

    def grad_block(source):
        for half in range(BLOCK // CH):
            part = pl.ds(pl.multiple_of(source * BLOCK + half * CH, CH), CH)
            gs_buf[part] = (scale_buf[part] * g_rows[part].astype(F32)).astype(BF)
        part = pl.ds(pl.multiple_of(source * BLOCK, BLOCK), BLOCK)
        acc[...] += tn(q_buf[part], spread(gs_buf[part]))

    att_out = []

    def send_out(d):
        to = lax.rem(z + d, NHEAD)
        copy = pltpu.make_async_remote_copy(
            src_ref=att_buf.at[pl.ds(to * BLK, BLK)],
            dst_ref=att_out_buf.at[:, z],
            send_sem=z_send.at[NHEAD + d],
            recv_sem=z_recv.at[NHEAD + d],
            device_id={"head": to},
            device_id_type=MESH,
        )
        copy.start()
        att_out.append(copy)

    for copy in grad_in[:HOLD]:
        copy.wait_recv()
    for d in SEND_ORDER[:2]:
        send_out(d)
    own_grad.wait()
    grad_block(z)
    for i, d in enumerate(SEND_ORDER):
        if i >= HOLD:
            grad_in[i].wait_recv()
        for e in SEND_ORDER[i + 2 : i + 2 + 1]:
            send_out(e)
        grad_block(lax.rem(z + NHEAD - d, NHEAD))

    gstate_buf[...] = stack(acc[...])
    scatter_pieces(gstate_buf, gpiece_in, 2)

    def query_grad(c):
        g = gs_buf[rows(c)]
        prefix = (prefix_buf[...].astype(F32) + k_run[c]).astype(BF)
        scores = nt(g, v_buf[rows(c)]).astype(BF) * tri_mask[...]
        total = nt(spread(g), wide(prefix)) + nn(scores, k_buf[rows(c)])
        qg_buf[rows(c)] = total.astype(BF)

    each_chunk(query_grad, 8)

    wait_pieces(gpiece_in, scan_recv.at[2])

    def scan_down(i, run):
        j = NSEQ - 1 - i
        gpiece_out[j] = run.astype(BF)
        return run + gpiece_in[j]

    lax.fori_loop(0, NSEQ, scan_down, jnp.zeros((PIECE, D), F32))
    return_pieces(gpiece_out, suffix_buf, 3)

    acc[...] = jnp.zeros_like(acc)

    def local_key_value(i):
        c = NCH - 1 - i
        g, q = gs_buf[rows(c)], q_buf[rows(c)]
        after = acc[...].astype(BF)
        acc[...] += tn(q, spread(g))
        scores_t = nt(v_buf[rows(c)], g).astype(BF) * tri_mask_t[...]
        kg_loc[rows(c)] = nn(scores_t, q) + nt(spread(v_buf[rows(c)]), after)
        vg_loc[rows(c)] = nn(within_t[c], g) + nn(spread(k_buf[rows(c)]), stack(after))

    each_chunk(local_key_value, 8)
    wait_rows(suffix_buf, scan_recv.at[3])

    def key_value(c):
        suffix = suffix_buf[...]
        kg = kg_loc[rows(c)] + nt(spread(v_buf[rows(c)]), wide(suffix))
        kg_buf[rows(c)] = kg.astype(BF)
        vg = vg_loc[rows(c)] + nn(spread(k_buf[rows(c)]), suffix)
        vg_buf[rows(c)] = vg.astype(BF)

    each_chunk(key_value, 8)

    wait_rows(state_buf, scan_send.at[0])
    wait_pieces(piece_out, scan_send.at[1])
    wait_rows(gstate_buf, scan_send.at[2])
    wait_pieces(gpiece_out, scan_send.at[3])
    for copy in grad_in:
        copy.wait_send()
    own_att.wait()
    for copy in att_out:
        copy.wait()


def store_kernel(*refs):
    sources, targets, sem = refs[:4], refs[4:8], refs[8]
    copies = [pltpu.make_async_copy(sources[i], targets[i], sem.at[i]) for i in range(4)]
    for copy in copies:
        copy.start()
    for copy in copies:
        copy.wait()


def per_device(queries, key_vectors, value_vectors, out_grad):
    hbm = pl.BlockSpec(memory_space=pltpu.HBM)
    vm = pltpu.VMEM
    in_vmem = pl.BlockSpec(memory_space=vm)
    dma = pltpu.SemaphoreType.DMA
    held = pl.pallas_call(
        kernel,
        out_shape=(vm((BLK, NHEAD, HL, D), BF), vm((ROWS, D), BF), vm((ROWS, D), BF), vm((ROWS, D), BF)),
        in_specs=[hbm] * 4,
        out_specs=[in_vmem] * 4,
        scratch_shapes=[
            vm((ROWS, D), BF), vm((ROWS, D), BF), vm((ROWS, D), BF),
            vm((TOK, HL, D), BF), vm((ROWS, D), BF), vm((TOK, HL, D), BF),
            vm((ROWS, D), F32), vm((ROWS, D), F32), vm((ROWS, D), F32),
            vm((NCH, HL * D, D), F32), vm((NCH, CH, CH), BF), vm((ROWS, D), F32),
            vm((BLOCK, HL * D), BF), vm((CH, CH), BF), vm((CH, CH), BF),
            vm((D, HL * D), F32),
            vm((HL * D, D), F32), vm((NSEQ, PIECE, D), F32), vm((NSEQ, PIECE, D), BF), vm((HL * D, D), BF),
            vm((HL * D, D), F32), vm((NSEQ, PIECE, D), F32), vm((NSEQ, PIECE, D), BF), vm((HL * D, D), BF),
            dma((3,)), dma((2 * NHEAD,)), dma((2 * NHEAD,)), dma((2,)), dma((4,)), dma((4,)),
            pltpu.SemaphoreType.REGULAR, pltpu.SemaphoreType.REGULAR,
        ],
        compiler_params=pltpu.CompilerParams(
            collective_id=0, has_side_effects=True, vmem_limit_bytes=56 * 2**20
        ),
        cost_estimate=pl.CostEstimate(flops=16 * 10**9, bytes_accessed=8 * 2**20, transcendentals=0),
        name="attend",
    )(
        queries.reshape(ROWS, D),
        key_vectors.reshape(ROWS, D),
        value_vectors.reshape(ROWS, D),
        out_grad.reshape(BLK, NHEAD, HL, D),
    )
    att, qg, kg, vg = pl.pallas_call(
        store_kernel,
        out_shape=[jax.ShapeDtypeStruct(x.shape, x.dtype) for x in held],
        in_specs=[pl.BlockSpec(memory_space=pl.ANY)] * 4,
        out_specs=[hbm] * 4,
        scratch_shapes=[dma((4,))],
        compiler_params=pltpu.CompilerParams(vmem_limit_bytes=2**20),
        name="store",
    )(*held)
    shape = (TOK, HL, D)
    return (att.reshape(BLK, NHEAD * HL, D), qg.reshape(shape), kg.reshape(shape), vg.reshape(shape))


def solution(mesh):
    return jax.shard_map(
        per_device,
        mesh=mesh,
        in_specs=(
            P("seq", "head", None),
            P("seq", "head", None),
            P("seq", "head", None),
            P(("seq", "head"), None, None),
        ),
        out_specs=(
            P(("seq", "head"), None, None),
            P("seq", "head", None),
            P("seq", "head", None),
            P("seq", "head", None),
        ),
        check_vma=False,
    )
```
